256 devices in a mesh: sub: 2 (over core), row: 16 (over y, x), col: 8 (over z).
Axes of the slice: x: 4, y: 4, z: 8, core: 2. Of those that a mesh axis runs over, the one named last changes fastest.
Arguments:
- front: bfloat16 [2048, 102400], P('row', ('sub', 'col')), may hold values from -6 to 6
- child_update: bfloat16 [2048, 131072], P('row', ('sub', 'col')), may hold values from -6 to 6
- col_map: int32 [1024], P(('sub', 'col')), may hold values from 0 to 799, as said below
- pivots: int32 [2, 512], replicated, may hold values from 0 to 511, each once within a row
- diag_inverse: float32 [2, 512, 512], replicated, may hold values from -0.01171875 to 0.01171875
- ranks: int32 [2, 16], P(None, 'row'), may hold values from 1 to 64
- bases: bfloat16 [64, 2048], P(None, 'row'), may hold values from -0.5 to 0.5
Outputs:
- front_out: bfloat16 [2048, 102400], P('row', ('sub', 'col'))
- coefficients: bfloat16 [2, 16, 64, 512], P(None, 'row')
The draws below stay inside these ranges and needn't reach their ends.
Inputs may be any that keep to these rules, and one draw needn't show every extreme that they name: `col_map`: within each half of the array (one child) the values are distinct. Each aligned run of 64 entries (one device's blocks) holds, for every o from 0 to 15, exactly 4 values v with o * 50 <= v < (o + 1) * 50.
All inputs are finite; a program needn't handle non-finite values.
Results may differ from the reference program's by a relative error of at most 0.011.
Values may be sent and summed in bfloat16 or wider, within the bound.
A program may use at most 128 MiB of HBM per device.

```python
import jax
import jax.numpy as jnp
from jax import lax

NF = 102400
BS = 128
P_SIZE = 512
NPAN = 2
RMAX = 64
SENDS = 4
OWNERS = 16
PB = 50
KB = 64
WR = 2048
NBR = 16
CHILD_COLS = 131072


def draw_col_map(key, part):
    key = jax.random.fold_in(key, 7)
    first_key, second_key = jax.random.split(key)
    sources = OWNERS // 2
    picks = jax.vmap(lambda single: jax.random.permutation(single, PB))(jax.random.split(first_key, 2 * OWNERS))
    picks = picks[:, :sources * SENDS].astype(jnp.int32).reshape(2, OWNERS, sources, SENDS)
    owner_base = (jnp.arange(OWNERS, dtype=jnp.int32) * PB).reshape(1, OWNERS, 1, 1)
    block_ids = (picks + owner_base).transpose(0, 2, 1, 3).reshape(2 * sources, KB)
    shuffle = jax.vmap(lambda single: jax.random.permutation(single, KB))(jax.random.split(second_key, 2 * sources))
    return jnp.take_along_axis(block_ids, shuffle.astype(jnp.int32), axis=1).reshape(-1).astype(jnp.int32)


def with_ends(drawn, rng, smallest, high):
    longest = drawn.shape.index(max(drawn.shape))
    spots = []
    for shift in (0, 1):
        where = [jax.random.randint(jax.random.fold_in(rng, axis), (), 0, length) for axis, length in enumerate(drawn.shape)]
        where[longest] = (where[longest] + shift) % drawn.shape[longest]
        spots.append(tuple(where))
    return drawn.at[spots[0]].set(smallest).at[spots[1]].set(high)


def levels(rng, dims, cuts, low, largest):
    level, own = 1.0, jax.random.fold_in(rng, 6)
    for position, shards_of in cuts:
        draws = jnp.exp(jax.random.uniform(jax.random.fold_in(own, position), (shards_of,), jnp.float32, low / len(cuts), largest / len(cuts)))
        level = level * jnp.repeat(draws, dims[position] // shards_of).reshape([-1 if axis == position else 1 for axis in range(len(dims))])
    return level


def normal_values(rng, shape, width, limit, pieces=(), kind=jnp.bfloat16):
    entries = width * jax.random.normal(rng, shape, jnp.float32)
    if pieces:
        entries = entries * levels(rng, shape, pieces, -0.22, 0.18)
    return jnp.clip(entries, -limit, limit).astype(kind)


def setup_inputs(seed: int = 0) -> dict:
    splits = jax.random.split(jax.random.key(seed), 8)
    front = normal_values(splits[0], (WR, NF), 1.0, 6.0, ((0, 16), (1, 16)))
    child_update = normal_values(splits[1], (WR, CHILD_COLS), 1.0, 6.0, ((0, 16), (1, 16)))
    col_map = draw_col_map(jax.random.fold_in(splits[7], 71), 0)
    pivots = jax.vmap(lambda own: jax.random.permutation(own, P_SIZE))(jax.random.split(splits[3], NPAN)).reshape((NPAN, P_SIZE)).astype(jnp.int32)
    diag_inverse = normal_values(splits[4], (NPAN, P_SIZE, P_SIZE), (P_SIZE * P_SIZE) ** -0.5, 0.01171875, (), jnp.float32)
    ranks = with_ends(jax.random.randint(splits[5], (NPAN, NBR), 1, RMAX + 1), jax.random.fold_in(splits[5], 1), 1, RMAX).astype(jnp.int32)
    bases = normal_values(splits[6], (RMAX, WR), BS ** -0.5, 0.5, ((1, 16),))
    return dict(front=front, child_update=child_update, col_map=col_map, pivots=pivots, diag_inverse=diag_inverse, ranks=ranks, bases=bases)


def reference(front, child_update, col_map, pivots, diag_inverse, ranks, bases):
    row_total = front.shape[0]
    block_total = NF // BS
    row_blocks = row_total // BS
    child_blocks = child_update.astype(jnp.float32).reshape(row_total, col_map.shape[0], BS)
    front_work = front.astype(jnp.float32).reshape(row_total, block_total, BS)
    front_work = front_work.at[:, col_map.astype(jnp.int32), :].add(child_blocks)
    front_work = front_work.reshape(row_total, NF)
    global_rows = jnp.arange(row_total, dtype=jnp.int32)
    coefficient_list = []
    for step in range(NPAN):
        rank_mask = (jnp.arange(RMAX, dtype=jnp.int32)[:, None] < ranks[step][None, :]).astype(jnp.float32)
        rank_basis = bases.astype(jnp.float32).reshape(RMAX, row_blocks, BS) * rank_mask[:, :, None]
        lower = jnp.dot(front_work[:, step * P_SIZE:(step + 1) * P_SIZE], diag_inverse[step], precision=lax.Precision.HIGHEST)
        coefficients = jnp.einsum("rnb,nbp->nrp", rank_basis, lower.reshape(row_blocks, BS, P_SIZE), precision=lax.Precision.HIGHEST).astype(jnp.bfloat16)
        upper = front_work[step * P_SIZE + pivots[step].astype(jnp.int32), :].astype(jnp.bfloat16)
        reduced = jnp.einsum("nrp,pc->nrc", coefficients.astype(jnp.float32), upper.astype(jnp.float32)).astype(jnp.bfloat16)
        update = jnp.einsum("rnb,nrc->nbc", rank_basis, reduced.astype(jnp.float32)).reshape(row_total, NF)
        below = (global_rows >= (step + 1) * P_SIZE)[:, None]
        front_work = front_work - jnp.where(below, update, jnp.float32(0.0))
        coefficient_list.append(coefficients)
    return front_work.astype(jnp.bfloat16), jnp.stack(coefficient_list)
```

```python
import functools

import jax
import jax.numpy as jnp
from jax import lax
from jax.experimental import pallas as pl
from jax.experimental.pallas import tpu as pltpu
from jax.sharding import PartitionSpec as P

BS = 128
PW = 512
RM = 64
ROWS = 128
COLS = 6400
PB = 50
KB = 64
NO = 16
ZS = 8
NCH = 4
RC = ROWS // NCH
WORKERS = (0, 1, 2, 3, 8, 9, 10, 11, 12, 13)
NW = len(WORKERS)
WC = COLS // NW
F32 = jnp.float32
BF16 = jnp.bfloat16
HIGH = lax.Precision.HIGHEST


def nt(a, b):
    return lax.dot_general(a, b, (((1,), (1,)), ((), ())), preferred_element_type=F32)


def mm(a, b):
    return jnp.dot(a, b, preferred_element_type=F32)


def mm_high(a, b):
    return jnp.dot(a, b, preferred_element_type=F32, precision=HIGH)


def transposed(a):
    return a.astype(F32).T


def kernel(
    cm, piv, ranks, bases, child, front, inv, out, coef_out,
    child_v, childs, front_v, inv_v, outbuf, recvs, plc_out, plc_in, arr_v, arr_s, src_v, src_s,
    work, fb, p1, u0p, coef, gmsg, g0, g1, u, r0, r1, rbuf, outv,
    s_child, s_load, s_idx, sa, ra, sp, rp, su, ru, sc, rcv, sg, rg, ss, rs, sr, rr, so, s_coef, s_self,
):
    s, r, c = lax.axis_index("sub"), lax.axis_index("row"), lax.axis_index("col")
    o = s * ZS + c

    def at_owner(q):
        return {"sub": q // ZS, "col": lax.rem(q, ZS)}

    def at_row(i):
        return {"row": jnp.int32(i)}

    def remote(src, dst, send, recv, dev):
        return pltpu.make_async_remote_copy(
            src_ref=src, dst_ref=dst, send_sem=send, recv_sem=recv, device_id=dev,
            device_id_type=pl.DeviceIdType.MESH,
        )

    def arrived(dst, sem):
        pltpu.make_async_copy(dst, dst, sem).wait()

    loads = []
    for ch in range(NCH):
        rows = pl.ds(ch * RC, RC)
        loads.append(pltpu.make_async_copy(child.at[rows, :], child_v.at[ch], s_child.at[ch]))
        loads[-1].start()
    front_load = pltpu.make_async_copy(front, front_v, s_load.at[0])
    front_load.start()
    inv_load = pltpu.make_async_copy(inv, inv_v, s_load.at[1])
    inv_load.start()

    barrier = pltpu.get_barrier_semaphore()

    @pl.loop(1, 16)
    def _(k):
        pl.semaphore_signal(
            barrier, inc=1, device_id=at_owner(lax.rem(o + k, NO)), device_id_type=pl.DeviceIdType.MESH
        )
        pl.semaphore_signal(
            barrier, inc=1, device_id=at_row(lax.rem(r + k, 16)), device_id_type=pl.DeviceIdType.MESH
        )

    i0 = lax.broadcasted_iota(jnp.int32, (KB, KB), 0)
    i1 = lax.broadcasted_iota(jnp.int32, (KB, KB), 1)
    along = jnp.broadcast_to(cm[...], (KB, KB))
    down = jnp.sum(jnp.where(i0 == i1, along, 0), axis=1, keepdims=True)
    t_along = (along * 1311) >> 16
    t_down = (down * 1311) >> 16
    slot = jnp.sum(jnp.where((t_along == t_down) & (i1 < i0), 1, 0), axis=1, keepdims=True)
    match = (4 * t_down + slot) == i1
    arrange = jnp.max(jnp.where(match, i0, 0), axis=0, keepdims=True)
    places = jnp.sum(jnp.where(match, down - PB * t_down, 0), axis=0, keepdims=True)
    arr_v[...] = jnp.zeros_like(arr_v)
    arr_v[:, 0:KB] = jnp.broadcast_to(arrange, (8, KB))
    plc_out[...] = jnp.zeros_like(plc_out)
    plc_out[:, 0:KB] = jnp.broadcast_to(places, (8, KB))
    idx_load = pltpu.make_async_copy(arr_v, arr_s, s_idx.at[0])
    idx_load.start()
    plc_in[o] = plc_out[...]
    for ch in range(NCH):
        recvs[ch][0] = jnp.zeros((RC, BS), BF16)
    idx_load.wait()
    pl.semaphore_wait(barrier, 30)

    def send_places(q):
        return remote(plc_out, plc_in.at[o], sp.at[q], rp.at[o], at_owner(q))

    def send_blocks(ch, q):
        return remote(
            outbuf.at[ch, pl.ds(4 * q, 4)], recvs[ch].at[pl.ds(1 + 4 * o, 4)], sa.at[ch, q], ra.at[ch, o],
            at_owner(q),
        )

    def pack(ch, q):
        for j in range(4):
            outbuf[ch, 4 * q + j] = childs[ch][arr_s[0, 4 * q + j]]

    @pl.loop(1, NO)
    def _(k):
        send_places(lax.rem(o + k, NO)).start()

    for ch in range(NCH):
        loads[ch].wait()

        @pl.loop(0, KB, unroll=8)
        def _(j, ch=ch):
            childs[ch][j] = child_v[ch, :, pl.ds(pl.multiple_of(j * BS, BS), BS)]

    for ch in range(NCH):
        pack(ch, 0)

        @pl.when(o != 0)
        def _(ch=ch):
            send_blocks(ch, 0).start()

    for ch in range(NCH):

        @pl.loop(0, NO)
        def _(t, ch=ch):
            step = t // 2
            shift = jnp.where(lax.rem(step, 2) == 1, (step + 1) // 2, ZS - step // 2)
            q = lax.rem(s + lax.rem(t, 2), 2) * ZS + lax.rem(c + shift, ZS)

            @pl.when(q != 0)
            def _():
                pack(ch, q)

                @pl.when(q != o)
                def _():
                    send_blocks(ch, q).start()

        for j in range(4):
            recvs[ch][1 + 4 * o + j] = outbuf[ch, 4 * o + j]

    @pl.loop(1, NO)
    def _(k):
        q = lax.rem(o + k, NO)
        arrived(plc_in.at[q], rp.at[q])

    ip = lax.broadcasted_iota(jnp.int32, (56, BS), 0)
    lane = lax.broadcasted_iota(jnp.int32, (56, BS), 1)
    mine = (lane >= 4 * o) & (lane < 4 * o + 4)
    for half in range(2):
        found = jnp.zeros((56, BS), jnp.int32)
        for q in range(half * ZS, (half + 1) * ZS):
            hit = mine & (plc_in[q, 0:1, :] == ip)
            found = jnp.maximum(found, jnp.where(hit, 4 * q + 1 + lane - 4 * o, 0))
        src_v[half] = jnp.broadcast_to(jnp.max(found, axis=1, keepdims=True), (56, BS))
    src_load = pltpu.make_async_copy(src_v, src_s, s_idx.at[1])
    src_load.start()
    front_load.wait()
    src_load.wait()

    def add_blocks(ch, first, last):
        rows = pl.ds(ch * RC, RC)

        @pl.loop(first, last)
        def _(p):
            at = pl.ds(pl.multiple_of(p * BS, BS), BS)
            one = recvs[ch][src_s[0, p, 0]].astype(F32)
            two = recvs[ch][src_s[1, p, 0]].astype(F32)
            total = front_v[rows, at].astype(F32) + one + two
            work[rows, at] = total
            fb[rows, at] = total.astype(BF16)

    def wait_blocks(ch):
        @pl.loop(1, NO)
        def _(k):
            q = lax.rem(o + k, NO)
            arrived(recvs[ch].at[pl.ds(1 + 4 * q, 4)], ra.at[ch, q])

    def send_rows(ch, w):
        src = fb.at[pl.ds(ch * RC, RC), pl.ds(w * WC, WC)]
        dst = u.at[pl.ds(pl.multiple_of(r * ROWS + ch * RC, RC), RC), :]
        return src, dst

    def scatter(ch):
        for w, row in enumerate(WORKERS):
            src, dst = send_rows(ch, w)

            @pl.when((r < 8) & (r == row))
            def _():
                pltpu.make_async_copy(src, dst, rs.at[ch, lax.rem(r, 8)]).start()

            @pl.when((r < 8) & (r != row))
            def _():
                remote(src, dst, ss.at[ch, w], rs.at[ch, lax.rem(r, 8)], at_row(row)).start()

    rank_row = lax.broadcasted_iota(jnp.int32, (RM, BS), 0)

    def basis(k):
        return jnp.where(rank_row < ranks[k, 0], bases[...].astype(F32), 0.0)

    def order(k):
        ids = lax.broadcasted_iota(jnp.int32, (PW, PW), 0)
        one_hot = jnp.where(piv[k : k + 1, :] == ids, 1.0, 0.0).astype(BF16)
        gmsg[k, :, 0:PW] = nt(coef[k], one_hot).astype(BF16)
        gmsg[k, :, PW : PW + BS] = basis(k).astype(BF16)

    def send_coef(k, q):
        return remote(coef.at[k], coef.at[k], sc.at[k, q], rcv.at[k], at_owner(q))

    def send_panel(i):
        return remote(
            fb.at[:, pl.ds(PW, PW)], u0p.at[pl.ds(pl.multiple_of(lax.rem(r, 4) * ROWS, ROWS), ROWS), :],
            su.at[i], ru.at[lax.rem(r, 4)], at_row(i),
        )

    @pl.when(o == 0)
    def _():
        for ch in range(NCH):
            wait_blocks(ch)
        for ch in range(NCH):
            add_blocks(ch, 0, 8)

        @pl.when(r < 4)
        def _():
            for i in range(4, 16):
                send_panel(i).start()

        inv_load.wait()
        coef[0] = mm_high(mm_high(basis(0), work[:, 0:PW]), inv_v[0]).astype(BF16)

        @pl.loop(1, NO)
        def _(q):
            send_coef(0, q).start()

        order(0)
        for ch in range(NCH):
            add_blocks(ch, 8, PB)
        for ch in range(NCH):
            scatter(ch)

        p1[...] = work[:, PW : 2 * PW]

        @pl.when(r >= 4)
        def _():
            for i in range(4):
                arrived(u0p.at[pl.ds(i * ROWS, ROWS), :], ru.at[i])
            reduced = mm(gmsg[0, :, 0:PW], u0p[...]).astype(BF16)
            p1[...] = p1[...] - mm(transposed(basis(0)).astype(BF16), reduced)

        coef[1] = mm_high(mm_high(basis(1), p1[...]), inv_v[1]).astype(BF16)

        @pl.loop(1, NO)
        def _(q):
            send_coef(1, q).start()

        order(1)

    @pl.when(o != 0)
    def _():
        inv_load.wait()
        arrived(coef.at[0], rcv.at[0])
        order(0)

    def send_order(k, w):
        first = 4 * (k + 1)
        at = pl.ds(pl.multiple_of(jnp.maximum(r - first, 0) * RM, RM), RM)
        return gmsg.at[k], (g0, g1)[k].at[at, :]

    def share(k):
        for w, row in enumerate(WORKERS):
            src, dst = send_order(k, w)

            @pl.when((r >= 4 * (k + 1)) & (r == row))
            def _():
                pltpu.make_async_copy(src, dst, rg.at[k, r]).start()

            @pl.when((r >= 4 * (k + 1)) & (r != row))
            def _():
                remote(src, dst, sg.at[k, w], rg.at[k, r], at_row(row)).start()

    share(0)

    @pl.when(o != 0)
    def _():
        arrived(coef.at[1], rcv.at[1])
        order(1)

    share(1)
    coef_copy = pltpu.make_async_copy(coef, coef_out, s_coef)
    coef_copy.start()

    @pl.when(o != 0)
    def _():
        for ch in range(NCH):
            wait_blocks(ch)
            add_blocks(ch, 0, PB)
            scatter(ch)

    w_me = jnp.int32(0)
    is_worker = r < 0
    for w, row in enumerate(WORKERS):
        w_me = jnp.where(r == row, w, w_me)
        is_worker = is_worker | (r == row)
    my_cols = pl.ds(pl.multiple_of(w_me * WC, BS), WC)

    def send_reduced(k, i):
        src = (r0, r1)[k].at[pl.ds((i - 4 * (k + 1)) * RM, RM), :]
        dst = rbuf.at[pl.ds(k * RM, RM), my_cols]
        return src, dst

    def give(k):
        for i in range(4 * (k + 1), 16):
            src, dst = send_reduced(k, i)

            @pl.when(r == i)
            def _():
                pltpu.make_async_copy(src, dst, rr.at[k, w_me]).start()

            @pl.when(r != i)
            def _():
                remote(src, dst, sr.at[k, i], rr.at[k, w_me], at_row(i)).start()

    @pl.when(is_worker)
    def _():
        for i in range(4, 16):
            arrived(g0.at[pl.ds((i - 4) * RM, RM), :], rg.at[0, i])
        for ch in range(NCH):
            for i in range(4):
                arrived(u.at[pl.ds(i * ROWS + ch * RC, RC), :], rs.at[ch, i])

        @pl.loop(0, 3)
        def _(t):
            at = pl.ds(pl.multiple_of(t * 256, 256), 256)
            r0[at, :] = mm(g0[at, 0:PW], u[0:PW, :]).astype(BF16)

        give(0)
        for ch in range(NCH):
            for i in range(4, 8):
                arrived(u.at[pl.ds(i * ROWS + ch * RC, RC), :], rs.at[ch, i])
        for i in range(4):
            b_t = transposed(g0[i * RM : (i + 1) * RM, PW : PW + BS]).astype(BF16)
            rows = pl.ds(PW + i * ROWS, ROWS)
            change = mm(b_t, r0[i * RM : (i + 1) * RM, :])
            u[rows, :] = (u[rows, :].astype(F32) - change).astype(BF16)
        for i in range(8, 16):
            arrived(g1.at[pl.ds((i - 8) * RM, RM), :], rg.at[1, i])

        @pl.loop(0, 2)
        def _(t):
            at = pl.ds(pl.multiple_of(t * 256, 256), 256)
            r1[at, :] = mm(g1[at, 0:PW], u[PW : 2 * PW, :]).astype(BF16)

        give(1)

    def write(w, src):
        at = pl.ds(w * WC, WC)
        return pltpu.make_async_copy(src.at[:, at], out.at[:, at], so.at[w])

    @pl.when(r < 4)
    def _():
        for w in range(NW):
            write(w, fb).start()

    @pl.when((r >= 4) & (r < 8))
    def _():
        b_t = transposed(basis(0)).astype(BF16)
        for w in range(NW):
            at = pl.ds(w * WC, WC)
            arrived(rbuf.at[pl.ds(0, RM), at], rr.at[0, w])
            outv[:, at] = (work[:, at] - mm(b_t, rbuf[0:RM, at])).astype(BF16)
            write(w, outv).start()

    @pl.when(r >= 8)
    def _():
        b_t = transposed(jnp.concatenate([basis(0), basis(1)], axis=0)).astype(BF16)
        for w in range(NW):
            at = pl.ds(w * WC, WC)
            for k in range(2):
                arrived(rbuf.at[pl.ds(k * RM, RM), at], rr.at[k, w])
            outv[:, at] = (work[:, at] - mm(b_t, rbuf[:, at])).astype(BF16)
            write(w, outv).start()

    for w in range(NW):
        write(w, outv).wait()
    coef_copy.wait()

    @pl.loop(1, NO)
    def _(k):
        q = lax.rem(o + k, NO)
        send_places(q).wait_send()
        for ch in range(NCH):
            send_blocks(ch, q).wait_send()

        @pl.when(o == 0)
        def _():
            for j in range(2):
                send_coef(j, q).wait_send()

    @pl.when((o == 0) & (r < 4))
    def _():
        for i in range(4, 16):
            send_panel(i).wait_send()

    for w, row in enumerate(WORKERS):
        for ch in range(NCH):
            src, dst = send_rows(ch, w)

            @pl.when((r < 8) & (r != row))
            def _():
                remote(src, dst, ss.at[ch, w], rs.at[ch, lax.rem(r, 8)], at_row(row)).wait_send()

        for k in range(2):
            src, dst = send_order(k, w)

            @pl.when((r >= 4 * (k + 1)) & (r != row))
            def _():
                remote(src, dst, sg.at[k, w], rg.at[k, r], at_row(row)).wait_send()

    for k in range(2):
        for i in range(4 * (k + 1), 16):
            src, dst = send_reduced(k, i)

            @pl.when(is_worker & (r != i))
            def _():
                remote(src, dst, sr.at[k, i], rr.at[k, w_me], at_row(i)).wait_send()


def local(front, child_update, col_map, pivots, diag_inverse, ranks, bases):
    vmem, smem, anywhere = (
        pl.BlockSpec(memory_space=pltpu.VMEM), pl.BlockSpec(memory_space=pltpu.SMEM),
        pl.BlockSpec(memory_space=pl.ANY),
    )
    dma = pltpu.SemaphoreType.DMA
    scratch = [
        pltpu.VMEM((NCH, RC, KB * BS), BF16),
        [pltpu.VMEM((KB, RC, BS), BF16) for _ in range(NCH)],
        pltpu.VMEM((ROWS, COLS), BF16),
        pltpu.VMEM((2, PW, PW), F32),
        pltpu.VMEM((NCH, KB, RC, BS), BF16),
        [pltpu.VMEM((KB + 1, RC, BS), BF16) for _ in range(NCH)],
        pltpu.VMEM((8, BS), jnp.int32),
        pltpu.VMEM((NO, 8, BS), jnp.int32),
        pltpu.VMEM((8, BS), jnp.int32),
        pltpu.SMEM((8, BS), jnp.int32),
        pltpu.VMEM((2, 56, BS), jnp.int32),
        pltpu.SMEM((2, 56, BS), jnp.int32),
        pltpu.VMEM((ROWS, COLS), F32),
        pltpu.VMEM((ROWS, COLS), BF16),
        pltpu.VMEM((ROWS, PW), F32),
        pltpu.VMEM((PW, PW), BF16),
        pltpu.VMEM((2, RM, PW), BF16),
        pltpu.VMEM((2, RM, PW + BS), BF16),
        pltpu.VMEM((12 * RM, PW + BS), BF16),
        pltpu.VMEM((8 * RM, PW + BS), BF16),
        pltpu.VMEM((2 * PW, WC), BF16),
        pltpu.VMEM((12 * RM, WC), BF16),
        pltpu.VMEM((8 * RM, WC), BF16),
        pltpu.VMEM((2 * RM, COLS), BF16),
        pltpu.VMEM((ROWS, COLS), BF16),
        dma((NCH,)), dma((2,)), dma((2,)),
        dma((NCH, NO)), dma((NCH, NO)), dma((NO,)), dma((NO,)),
        dma((16,)), dma((4,)),
        dma((2, NO)), dma((2,)),
        dma((2, NW)), dma((2, 16)),
        dma((NCH, NW)), dma((NCH, 8)),
        dma((2, 16)), dma((2, NW)),
        dma((NW,)), dma(()), dma(()),
    ]
    front_out, coefficients = pl.pallas_call(
        kernel,
        out_shape=(
            jax.ShapeDtypeStruct((ROWS, COLS), BF16),
            jax.ShapeDtypeStruct((2, RM, PW), BF16),
        ),
        in_specs=[vmem, vmem, smem, vmem, anywhere, anywhere, anywhere],
        out_specs=(anywhere, anywhere),
        scratch_shapes=scratch,
        compiler_params=pltpu.CompilerParams(
            collective_id=0, has_side_effects=True, vmem_limit_bytes=50 * 1024 * 1024
        ),
        cost_estimate=pl.CostEstimate(flops=1_200_000_000, bytes_accessed=8_000_000, transcendentals=0),
    )(col_map.reshape(1, KB), pivots, ranks, bases, child_update, front, diag_inverse)
    return front_out, coefficients.reshape(2, 1, RM, PW)


def solution(mesh):
    return jax.shard_map(
        local,
        mesh=mesh,
        in_specs=(
            P("row", ("sub", "col")),
            P("row", ("sub", "col")),
            P(("sub", "col")),
            P(),
            P(),
            P(None, "row"),
            P(None, "row"),
        ),
        out_specs=(P("row", ("sub", "col")), P(None, "row", None, None)),
        check_vma=False,
    )
```

```python
import functools

import jax
import jax.numpy as jnp
from jax import lax
from jax.experimental import pallas as pl
from jax.experimental.pallas import tpu as pltpu
from jax.sharding import PartitionSpec as P

BS = 128
PW = 512
RM = 64
ROWS = 128
COLS = 6400
PB = 50
KB = 64
NO = 16
ZS = 8
NCH = 4
RC = ROWS // NCH
NW = 16
SHARES = ((0, 2, 3), (2, 8, 2), (8, 16, 4))
WC = 4 * BS
F32 = jnp.float32
BF16 = jnp.bfloat16
HIGH = lax.Precision.HIGHEST


def first_col(w):
    return pl.multiple_of(jnp.where(w < 8, 2 * w + jnp.minimum(w, 2), 4 * w - 14) * BS, BS)


def by_width(w, act):
    for start, end, blocks in SHARES:

        @pl.when((w >= start) & (w < end))
        def _():
            act(blocks * BS)


def nt(a, b):
    return lax.dot_general(a, b, (((1,), (1,)), ((), ())), preferred_element_type=F32)


def mm(a, b):
    return jnp.dot(a, b, preferred_element_type=F32)


def mm_high(a, b):
    return jnp.dot(a, b, preferred_element_type=F32, precision=HIGH)


def transposed(a):
    return a.astype(F32).T


def kernel(
    cm_h, piv_h, ranks_h, bases_h, child, front, inv, out, coef_out,
    cm, piv, ranks, bases, one_hot, child_v, childs, front_v, inv_v, outbuf, recvs, plc_out, plc_in, arr_v, arr_s, src_v, src_s,
    work, fb, p1, u0p, coef, gm0, gm1, g0, g1, u, r0, r1, rbuf, outv,
    s_child, s_load, s_idx, sa, ra, sp, rp, su, ru, sc, rcv, sg, rg, sf, ss, rs, sr, rr, so, s_coef,
):
    s, r, c = lax.axis_index("sub"), lax.axis_index("row"), lax.axis_index("col")
    o = s * ZS + c

    def at_owner(q):
        return {"sub": q // ZS, "col": lax.rem(q, ZS)}

    def at_row(i):
        return {"row": i}

    def remote(src, dst, send, recv, dev):
        return pltpu.make_async_remote_copy(
            src_ref=src, dst_ref=dst, send_sem=send, recv_sem=recv, device_id=dev,
            device_id_type=pl.DeviceIdType.MESH,
        )

    def arrived(dst, sem):
        pltpu.make_async_copy(dst, dst, sem).wait()

    small = []
    for i, (src, dst) in enumerate(((cm_h, cm), (piv_h, piv), (ranks_h, ranks), (bases_h, bases))):
        small.append(pltpu.make_async_copy(src, dst, s_load.at[2 + i]))
        small[-1].start()
    loads = []
    for ch in range(NCH):
        rows = pl.ds(ch * RC, RC)
        loads.append(pltpu.make_async_copy(child.at[rows, :], child_v.at[ch], s_child.at[ch]))
        loads[-1].start()
    front_load = pltpu.make_async_copy(front, front_v, s_load.at[0])
    front_load.start()
    inv_load = pltpu.make_async_copy(inv, inv_v, s_load.at[1])
    inv_load.start()

    barrier = pltpu.get_barrier_semaphore()

    @pl.loop(1, 16)
    def _(k):
        pl.semaphore_signal(
            barrier, inc=1, device_id=at_owner(lax.rem(o + k, NO)), device_id_type=pl.DeviceIdType.MESH
        )
        pl.semaphore_signal(
            barrier, inc=1, device_id=at_row(lax.rem(r + k, 16)), device_id_type=pl.DeviceIdType.MESH
        )

    small[0].wait()
    i0 = lax.broadcasted_iota(jnp.int32, (KB, KB), 0)
    i1 = lax.broadcasted_iota(jnp.int32, (KB, KB), 1)
    along = jnp.broadcast_to(cm[...], (KB, KB))
    down = jnp.sum(jnp.where(i0 == i1, along, 0), axis=1, keepdims=True)
    t_along = (along * 1311) >> 16
    t_down = (down * 1311) >> 16
    slot = jnp.sum(jnp.where((t_along == t_down) & (i1 < i0), 1, 0), axis=1, keepdims=True)
    match = (4 * t_down + slot) == i1
    arrange = jnp.max(jnp.where(match, i0, 0), axis=0, keepdims=True)
    places = jnp.sum(jnp.where(match, down - PB * t_down, 0), axis=0, keepdims=True)
    arr_v[...] = jnp.zeros_like(arr_v)
    arr_v[:, 0:KB] = jnp.broadcast_to(arrange, (8, KB))
    plc_out[...] = jnp.zeros_like(plc_out)
    plc_out[:, 0:KB] = jnp.broadcast_to(places, (8, KB))
    idx_load = pltpu.make_async_copy(arr_v, arr_s, s_idx.at[0])
    idx_load.start()
    plc_in[o] = plc_out[...]
    for ch in range(NCH):
        recvs[ch][0] = jnp.zeros((RC, BS), BF16)
    idx_load.wait()
    pl.semaphore_wait(barrier, 30)

    def send_places(q):
        return remote(plc_out, plc_in.at[o], sp.at[q], rp.at[o], at_owner(q))

    def send_blocks(ch, q):
        return remote(
            outbuf.at[ch, pl.ds(4 * q, 4)], recvs[ch].at[pl.ds(1 + 4 * o, 4)], sa.at[ch, q], ra.at[ch, o],
            at_owner(q),
        )

    def pack(ch, q):
        for j in range(4):
            outbuf[ch, 4 * q + j] = childs[ch][arr_s[0, 4 * q + j]]

    @pl.loop(1, NO)
    def _(k):
        send_places(lax.rem(o + k, NO)).start()

    for ch in range(NCH):
        loads[ch].wait()

        @pl.loop(0, KB, unroll=8)
        def _(j, ch=ch):
            childs[ch][j] = child_v[ch, :, pl.ds(pl.multiple_of(j * BS, BS), BS)]

    def send_chunk(ch):
        @pl.loop(0, NO)
        def _(t):
            if ch == 0:

                @pl.when(lax.rem(t, 4) == 0)
                def _():
                    for early in range(NCH):

                        @pl.when(t == 4 * early)
                        def _():
                            pack(early, 0)

                            @pl.when(o != 0)
                            def _():
                                send_blocks(early, 0).start()

            step = t // 2
            shift = jnp.where(lax.rem(step, 2) == 1, (step + 1) // 2, ZS - step // 2)
            q = lax.rem(s + lax.rem(t, 2), 2) * ZS + lax.rem(c + shift, ZS)

            @pl.when(q != 0)
            def _():
                pack(ch, q)

                @pl.when(q != o)
                def _():
                    send_blocks(ch, q).start()

        for j in range(4):
            recvs[ch][1 + 4 * o + j] = outbuf[ch, 4 * o + j]

    send_chunk(0)

    @pl.when(o == 0)
    def _():
        for ch in range(1, NCH):
            for j in range(4):
                recvs[ch][1 + j] = outbuf[ch, j]

    send_chunk(1)

    @pl.when(o != 0)
    def _():
        send_chunk(2)
        send_chunk(3)

    for load in small[1:]:
        load.wait()
    ids = lax.broadcasted_iota(jnp.int32, (PW, PW), 0)
    for k in range(2):
        one_hot[k] = jnp.where(piv[k : k + 1, :] == ids, 1.0, 0.0).astype(BF16)

    @pl.loop(1, NO)
    def _(k):
        q = lax.rem(o + k, NO)
        arrived(plc_in.at[q], rp.at[q])

    ip = lax.broadcasted_iota(jnp.int32, (56, BS), 0)
    lane = lax.broadcasted_iota(jnp.int32, (56, BS), 1)
    mine = (lane >= 4 * o) & (lane < 4 * o + 4)
    for half in range(2):
        found = jnp.zeros((56, BS), jnp.int32)
        for q in range(half * ZS, (half + 1) * ZS):
            hit = mine & (plc_in[q, 0:1, :] == ip)
            found = jnp.maximum(found, jnp.where(hit, 4 * q + 1 + lane - 4 * o, 0))
        src_v[half] = jnp.broadcast_to(jnp.max(found, axis=1, keepdims=True), (56, BS))
    src_load = pltpu.make_async_copy(src_v, src_s, s_idx.at[1])
    src_load.start()
    front_load.wait()
    src_load.wait()

    def add_blocks(ch, first, last):
        rows = pl.ds(ch * RC, RC)

        @pl.loop(first, last, unroll=2)
        def _(p):
            at = pl.ds(pl.multiple_of(p * BS, BS), BS)
            one = recvs[ch][src_s[0, p, 0]].astype(F32)
            two = recvs[ch][src_s[1, p, 0]].astype(F32)
            total = front_v[rows, at].astype(F32) + one + two
            work[rows, at] = total
            fb[rows, at] = total.astype(BF16)

    def wait_blocks(ch):
        @pl.loop(1, NO)
        def _(k):
            q = lax.rem(o + k, NO)
            arrived(recvs[ch].at[pl.ds(1 + 4 * q, 4)], ra.at[ch, q])

    def send_rows(ch, w, cols):
        src = fb.at[pl.ds(ch * RC, RC), pl.ds(first_col(w), cols)]
        dst = u.at[pl.ds(pl.multiple_of(r * ROWS + ch * RC, RC), RC), pl.ds(0, cols)]
        return src, dst

    def scatter(ch):
        @pl.when(r < 8)
        def _():
            @pl.loop(0, NW)
            def _(t):
                w = lax.rem(r + t, NW)

                def act(cols):
                    src, dst = send_rows(ch, w, cols)

                    @pl.when(w == r)
                    def _():
                        pltpu.make_async_copy(src, dst, rs.at[ch, lax.rem(r, 8)]).start()

                    @pl.when(w != r)
                    def _():
                        remote(src, dst, ss.at[ch, w], rs.at[ch, lax.rem(r, 8)], at_row(w)).start()

                by_width(w, act)

    rank_row = lax.broadcasted_iota(jnp.int32, (RM, BS), 0)

    def basis(k):
        return jnp.where(rank_row < ranks[0:1, k : k + 1], bases[...].astype(F32), 0.0)

    def order(k):
        ordered = nt(coef[k], one_hot[k]).astype(BF16)
        at = pl.ds(pl.multiple_of(jnp.maximum(r - 4 * (k + 1), 0) * RM, RM), RM)
        if k == 0:
            gm0[:, 0:PW] = ordered
            gm0[:, PW : PW + BS] = basis(k).astype(BF16)
        else:
            gm1[...] = ordered

        @pl.when(r >= 4 * (k + 1))
        def _():
            (g0, g1)[k][at, :] = (gm0, gm1)[k][...]

    def send_coef(k, q):
        return remote(coef.at[k], coef.at[k], sc.at[k, q], rcv.at[k], {"col": q})

    def send_pair(k):
        return remote(coef.at[k], coef.at[k], sc.at[k, 0], rcv.at[k], {"sub": 1 - s})

    def pass_coef(k):
        @pl.when(o == 0)
        def _():
            @pl.loop(1, ZS)
            def _(t):
                step = jnp.where(lax.rem(t, 2) == 1, ZS // 2 - t // 2, ZS // 2 + t // 2)
                send_coef(k, step).start()

        @pl.when(s == 0)
        def _():
            send_pair(k).start()

    def send_panel(i):
        return remote(
            fb.at[:, pl.ds(PW, PW)], u0p.at[pl.ds(pl.multiple_of(lax.rem(r, 4) * ROWS, ROWS), ROWS), :],
            su.at[i], ru.at[lax.rem(r, 4)], at_row(i),
        )

    def slot(k, i):
        return (g0, g1)[k].at[pl.ds(pl.multiple_of((i - 4 * (k + 1)) * RM, RM), RM), :]

    def send_order(k, w):
        at = pl.ds(pl.multiple_of(jnp.maximum(r - 4 * (k + 1), 0) * RM, RM), RM)
        return remote((gm0, gm1)[k], (g0, g1)[k].at[at, :], sg.at[k, w], rg.at[k, r], at_row(w))

    def sends_order(k, w):
        return (r >= 4 * (k + 1)) & (lax.rem(r, 2) == s) & (r != w)

    def share(k):
        @pl.loop(1, NW)
        def _(t):
            w = lax.rem(r + t, NW)

            @pl.when(sends_order(k, w))
            def _():
                send_order(k, w).start()

    def send_sibling(k, i):
        return remote(slot(k, i), slot(k, i), sf.at[k, i], rg.at[k, i], {"sub": 1 - s})

    def exchange(k):
        @pl.loop(4 * (k + 1), 16)
        def _(i):
            @pl.when((r != i) & (s == lax.rem(i, 2)))
            def _():
                arrived(slot(k, i), rg.at[k, i])
                send_sibling(k, i).start()

    def exchanged(k):
        @pl.loop(4 * (k + 1), 16)
        def _(i):
            @pl.when((r != i) & (s != lax.rem(i, 2)))
            def _():
                arrived(slot(k, i), rg.at[k, i])

    @pl.when(o == 0)
    def _():
        for ch in range(NCH):
            wait_blocks(ch)
        for ch in range(NCH):
            add_blocks(ch, 0, 8)

        @pl.when(r < 4)
        def _():
            @pl.loop(4, 16)
            def _(i):
                send_panel(i).start()

        inv_load.wait()
        coef[0] = mm_high(mm_high(basis(0), work[:, 0:PW]), inv_v[0]).astype(BF16)
        pass_coef(0)
        order(0)
        share(0)
        for ch in range(NCH):
            add_blocks(ch, 8, PB)
        p1[...] = work[:, PW : 2 * PW]

        @pl.when(r >= 4)
        def _():
            for i in range(4):
                arrived(u0p.at[pl.ds(i * ROWS, ROWS), :], ru.at[i])
            reduced = mm(gm0[:, 0:PW], u0p[...]).astype(BF16)
            p1[...] = p1[...] - mm(transposed(basis(0)).astype(BF16), reduced)

        coef[1] = mm_high(mm_high(basis(1), p1[...]), inv_v[1]).astype(BF16)
        pass_coef(1)
        send_chunk(2)
        send_chunk(3)
        order(1)
        share(1)
        for ch in range(NCH):
            scatter(ch)
        exchange(0)

    @pl.when(o != 0)
    def _():
        inv_load.wait()
        arrived(coef.at[0], rcv.at[0])
        pass_coef(0)
        order(0)
        share(0)
        for ch in range(NCH - 1):
            wait_blocks(ch)
            add_blocks(ch, 0, PB)
            scatter(ch)
        exchange(0)
        wait_blocks(NCH - 1)
        add_blocks(NCH - 1, 0, PB)
        scatter(NCH - 1)
        arrived(coef.at[1], rcv.at[1])
        pass_coef(1)
        order(1)
        share(1)

    coef_copy = pltpu.make_async_copy(coef, coef_out.at[:, 0], s_coef)
    coef_copy.start()

    def got_rows(first, last):
        def act(cols):
            @pl.loop(first, last)
            def _(i):
                for ch in range(NCH):
                    rows = pl.ds(pl.multiple_of(i * ROWS + ch * RC, RC), RC)
                    arrived(u.at[rows, pl.ds(0, cols)], rs.at[ch, i])

        by_width(r, act)

    def send_reduced(k, i, cols):
        src = (r0, r1)[k].at[pl.ds(pl.multiple_of((i - 4 * (k + 1)) * RM, RM), RM), pl.ds(0, cols)]
        dst = rbuf.at[pl.ds(k * RM, RM), pl.ds(first_col(r), cols)]
        return src, dst

    def give(k, first):
        def act(cols):
            @pl.loop(0, 4)
            def _(t):
                i = first + lax.rem(r + t, 4)
                src, dst = send_reduced(k, i, cols)

                @pl.when(r == i)
                def _():
                    pltpu.make_async_copy(src, dst, rr.at[k, r]).start()

                @pl.when(r != i)
                def _():
                    remote(src, dst, sr.at[k, i], rr.at[k, r], at_row(i)).start()

        by_width(r, act)

    exchanged(0)
    got_rows(0, 4)

    @pl.loop(0, 3)
    def _(t):
        at = pl.ds(pl.multiple_of(t * 256, 256), 256)
        r0[at, :] = mm(g0[at, 0:PW], u[0:PW, :]).astype(BF16)
        give(0, 4 + 4 * t)

    exchange(1)
    got_rows(4, 8)

    @pl.loop(0, 4)
    def _(i):
        ranks_at = pl.ds(pl.multiple_of(i * RM, RM), RM)
        b_t = transposed(g0[ranks_at, PW : PW + BS]).astype(BF16)
        rows = pl.ds(pl.multiple_of(PW + i * ROWS, ROWS), ROWS)
        u[rows, :] = (u[rows, :].astype(F32) - mm(b_t, r0[ranks_at, :])).astype(BF16)

    exchanged(1)

    @pl.loop(0, 2)
    def _(t):
        at = pl.ds(pl.multiple_of(t * 256, 256), 256)
        r1[at, :] = mm(g1[at, :], u[PW : 2 * PW, :]).astype(BF16)
        give(1, 8 + 4 * t)

    def each_part(act):
        @pl.loop(0, NW)
        def _(w):
            by_width(w, lambda cols: act(w, cols))

    def write(w, cols, src):
        at = pl.ds(first_col(w), cols)
        return pltpu.make_async_copy(src.at[:, at], out.at[:, at], so.at[w])

    @pl.when(r < 4)
    def _():
        each_part(lambda w, cols: write(w, cols, fb).start())

    def apply(count):
        b_t = transposed(jnp.concatenate([basis(0), basis(1)][:count], axis=0)).astype(BF16)

        def act(w, cols):
            at = pl.ds(first_col(w), cols)
            for k in range(count):
                arrived(rbuf.at[pl.ds(k * RM, RM), at], rr.at[k, w])
            outv[:, at] = (work[:, at] - mm(b_t, rbuf[0 : count * RM, at])).astype(BF16)
            write(w, cols, outv).start()

        each_part(act)

    @pl.when((r >= 4) & (r < 8))
    def _():
        apply(1)

    @pl.when(r >= 8)
    def _():
        apply(2)

    each_part(lambda w, cols: write(w, cols, outv).wait())
    coef_copy.wait()

    @pl.loop(1, NO)
    def _(k):
        q = lax.rem(o + k, NO)
        send_places(q).wait_send()
        for ch in range(NCH):
            send_blocks(ch, q).wait_send()

    @pl.when((o == 0) & (r < 4))
    def _():
        @pl.loop(4, 16)
        def _(i):
            send_panel(i).wait_send()

    for k in range(2):

        @pl.when(o == 0)
        def _():
            @pl.loop(1, ZS)
            def _(q):
                send_coef(k, q).wait_send()

        @pl.when(s == 0)
        def _():
            send_pair(k).wait_send()

        @pl.loop(0, NW)
        def _(w):
            @pl.when(sends_order(k, w))
            def _():
                send_order(k, w).wait_send()

        @pl.loop(4 * (k + 1), 16)
        def _(i):
            @pl.when((r != i) & (s == lax.rem(i, 2)))
            def _():
                send_sibling(k, i).wait_send()

        def sent(cols, k=k):
            @pl.loop(4 * (k + 1), 16)
            def _(i):
                src, dst = send_reduced(k, i, cols)

                @pl.when(r != i)
                def _():
                    remote(src, dst, sr.at[k, i], rr.at[k, r], at_row(i)).wait_send()

        by_width(r, sent)

    @pl.when(r < 8)
    def _():
        @pl.loop(1, NW)
        def _(t):
            w = lax.rem(r + t, NW)

            def act(cols):
                for ch in range(NCH):
                    src, dst = send_rows(ch, w, cols)
                    remote(src, dst, ss.at[ch, w], rs.at[ch, lax.rem(r, 8)], at_row(w)).wait_send()

            by_width(w, act)


def local(front, child_update, col_map, pivots, diag_inverse, ranks, bases):
    anywhere = pl.BlockSpec(memory_space=pl.ANY)
    dma = pltpu.SemaphoreType.DMA
    scratch = [
        pltpu.VMEM((1, KB), jnp.int32),
        pltpu.VMEM((2, PW), jnp.int32),
        pltpu.VMEM((1, 2), jnp.int32),
        pltpu.VMEM((RM, BS), BF16),
        pltpu.VMEM((2, PW, PW), BF16),
        pltpu.VMEM((NCH, RC, KB * BS), BF16),
        [pltpu.VMEM((KB, RC, BS), BF16) for _ in range(NCH)],
        pltpu.VMEM((ROWS, COLS), BF16),
        pltpu.VMEM((2, PW, PW), F32),
        pltpu.VMEM((NCH, KB, RC, BS), BF16),
        [pltpu.VMEM((KB + 1, RC, BS), BF16) for _ in range(NCH)],
        pltpu.VMEM((8, BS), jnp.int32),
        pltpu.VMEM((NO, 8, BS), jnp.int32),
        pltpu.VMEM((8, BS), jnp.int32),
        pltpu.SMEM((8, BS), jnp.int32),
        pltpu.VMEM((2, 56, BS), jnp.int32),
        pltpu.SMEM((2, 56, BS), jnp.int32),
        pltpu.VMEM((ROWS, COLS), F32),
        pltpu.VMEM((ROWS, COLS), BF16),
        pltpu.VMEM((ROWS, PW), F32),
        pltpu.VMEM((PW, PW), BF16),
        pltpu.VMEM((2, RM, PW), BF16),
        pltpu.VMEM((RM, PW + BS), BF16),
        pltpu.VMEM((RM, PW), BF16),
        pltpu.VMEM((12 * RM, PW + BS), BF16),
        pltpu.VMEM((8 * RM, PW), BF16),
        pltpu.VMEM((2 * PW, WC), BF16),
        pltpu.VMEM((12 * RM, WC), BF16),
        pltpu.VMEM((8 * RM, WC), BF16),
        pltpu.VMEM((2 * RM, COLS), BF16),
        pltpu.VMEM((ROWS, COLS), BF16),
        dma((NCH,)), dma((6,)), dma((2,)),
        dma((NCH, NO)), dma((NCH, NO)), dma((NO,)), dma((NO,)),
        dma((16,)), dma((4,)),
        dma((2, 8)), dma((2,)),
        dma((2, NW)), dma((2, 16)), dma((2, 16)),
        dma((NCH, NW)), dma((NCH, 8)),
        dma((2, 16)), dma((2, NW)),
        dma((NW,)), dma(()),
    ]
    return pl.pallas_call(
        kernel,
        out_shape=(
            jax.ShapeDtypeStruct((ROWS, COLS), BF16),
            jax.ShapeDtypeStruct((2, 1, RM, PW), BF16),
        ),
        in_specs=[anywhere] * 7,
        out_specs=(anywhere, anywhere),
        scratch_shapes=scratch,
        compiler_params=pltpu.CompilerParams(
            collective_id=0, has_side_effects=True, vmem_limit_bytes=60 * 1024 * 1024
        ),
        cost_estimate=pl.CostEstimate(flops=1_200_000_000, bytes_accessed=8_000_000, transcendentals=0),
    )(col_map.reshape(1, KB), pivots, ranks.reshape(1, 2), bases, child_update, front, diag_inverse)


def solution(mesh):
    return jax.shard_map(
        local,
        mesh=mesh,
        in_specs=(
            P("row", ("sub", "col")),
            P("row", ("sub", "col")),
            P(("sub", "col")),
            P(),
            P(),
            P(None, "row"),
            P(None, "row"),
        ),
        out_specs=(P("row", ("sub", "col")), P(None, "row", None, None)),
        check_vma=False,
    )
```

```python
import functools

import jax
import jax.numpy as jnp
from jax import lax
from jax.experimental import pallas as pl
from jax.experimental.pallas import tpu as pltpu
from jax.sharding import PartitionSpec as P

BS = 128
PW = 512
RM = 64
ROWS = 128
COLS = 6400
PB = 50
KB = 64
NO = 16
ZS = 8
NCH = 4
RC = ROWS // NCH
NW = 16
SHARES = ((0, 2, 3), (2, 8, 2), (8, 16, 4))
WC = 4 * BS
F32 = jnp.float32
BF16 = jnp.bfloat16
HIGH = lax.Precision.HIGHEST


def first_col(w):
    return pl.multiple_of(jnp.where(w < 8, 2 * w + jnp.minimum(w, 2), 4 * w - 14) * BS, BS)


def by_width(w, act):
    for start, end, blocks in SHARES:

        @pl.when((w >= start) & (w < end))
        def _():
            act(blocks * BS)


def nt(a, b):
    return lax.dot_general(a, b, (((1,), (1,)), ((), ())), preferred_element_type=F32)


def mm(a, b):
    return jnp.dot(a, b, preferred_element_type=F32)


def mm_high(a, b):
    return jnp.dot(a, b, preferred_element_type=F32, precision=HIGH)


def transposed(a):
    return a.astype(F32).T


def kernel(
    cm_h, piv_h, ranks_h, bases_h, child, front, inv, out, coef_out,
    cm, piv, ranks, bases, one_hot, child_v, childs, front_v, inv_v, outbuf, recvs, plc_out, plc_in, arr_v, arr_s, src_v, src_s,
    work, fb, p1, u0p, coef, gm0, gm1, g0, g1, u, r0, r1, rbuf, outv,
    s_child, s_load, s_idx, sa, ra, sp, rp, su, ru, sc, rcv, sg, rg, sf, ss, rs, sr, rr, so, s_coef,
):
    s, r, c = lax.axis_index("sub"), lax.axis_index("row"), lax.axis_index("col")
    o = s * ZS + c

    def at_owner(q):
        return {"sub": q // ZS, "col": lax.rem(q, ZS)}

    def at_row(i):
        return {"row": i}

    def remote(src, dst, send, recv, dev):
        return pltpu.make_async_remote_copy(
            src_ref=src, dst_ref=dst, send_sem=send, recv_sem=recv, device_id=dev,
            device_id_type=pl.DeviceIdType.MESH,
        )

    def arrived(dst, sem):
        pltpu.make_async_copy(dst, dst, sem).wait()

    small = []
    for i, (src, dst) in enumerate(((cm_h, cm), (piv_h, piv), (ranks_h, ranks), (bases_h, bases))):
        small.append(pltpu.make_async_copy(src, dst, s_load.at[2 + i]))
        small[-1].start()
    loads = []
    for ch in range(NCH):
        rows = pl.ds(ch * RC, RC)
        loads.append(pltpu.make_async_copy(child.at[rows, :], child_v.at[ch], s_child.at[ch]))
        loads[-1].start()
    front_load = pltpu.make_async_copy(front, front_v, s_load.at[0])
    front_load.start()
    inv_load = pltpu.make_async_copy(inv, inv_v, s_load.at[1])
    inv_load.start()

    barrier = pltpu.get_barrier_semaphore()

    @pl.loop(1, 16)
    def _(k):
        pl.semaphore_signal(
            barrier, inc=1, device_id=at_owner(lax.rem(o + k, NO)), device_id_type=pl.DeviceIdType.MESH
        )
        pl.semaphore_signal(
            barrier, inc=1, device_id=at_row(lax.rem(r + k, 16)), device_id_type=pl.DeviceIdType.MESH
        )

    small[0].wait()
    i0 = lax.broadcasted_iota(jnp.int32, (KB, KB), 0)
    i1 = lax.broadcasted_iota(jnp.int32, (KB, KB), 1)
    along = jnp.broadcast_to(cm[...], (KB, KB))
    down = jnp.sum(jnp.where(i0 == i1, along, 0), axis=1, keepdims=True)
    t_along = (along * 1311) >> 16
    t_down = (down * 1311) >> 16
    slot = jnp.sum(jnp.where((t_along == t_down) & (i1 < i0), 1, 0), axis=1, keepdims=True)
    match = (4 * t_down + slot) == i1
    arrange = jnp.max(jnp.where(match, i0, 0), axis=0, keepdims=True)
    places = jnp.sum(jnp.where(match, down - PB * t_down, 0), axis=0, keepdims=True)
    arr_v[...] = jnp.zeros_like(arr_v)
    arr_v[:, 0:KB] = jnp.broadcast_to(arrange, (8, KB))
    plc_out[...] = jnp.zeros_like(plc_out)
    plc_out[:, 0:KB] = jnp.broadcast_to(places, (8, KB))
    idx_load = pltpu.make_async_copy(arr_v, arr_s, s_idx.at[0])
    idx_load.start()
    plc_in[o] = plc_out[...]
    for ch in range(NCH):
        recvs[ch][0] = jnp.zeros((RC, BS), BF16)
    idx_load.wait()
    pl.semaphore_wait(barrier, 30)

    def send_places(q):
        return remote(plc_out, plc_in.at[o], sp.at[q], rp.at[o], at_owner(q))

    def send_blocks(ch, q):
        return remote(
            outbuf.at[ch, pl.ds(4 * q, 4)], recvs[ch].at[pl.ds(1 + 4 * o, 4)], sa.at[ch, q], ra.at[ch, o],
            at_owner(q),
        )

    def pack(ch, q):
        for j in range(4):
            outbuf[ch, 4 * q + j] = childs[ch][arr_s[0, 4 * q + j]]

    @pl.loop(1, NO)
    def _(k):
        send_places(lax.rem(o + k, NO)).start()

    for ch in range(NCH):
        loads[ch].wait()

        @pl.loop(0, KB, unroll=8)
        def _(j, ch=ch):
            childs[ch][j] = child_v[ch, :, pl.ds(pl.multiple_of(j * BS, BS), BS)]

    def send_chunk(ch):
        @pl.loop(0, NO)
        def _(t):
            step = t // 2
            base = 0 if ch == NCH - 1 else ZS // 2
            shift = jnp.where(lax.rem(step, 2) == 1, base + (step + 1) // 2, base + ZS - step // 2)
            q = lax.rem(s + lax.rem(t, 2), 2) * ZS + lax.rem(c + shift, ZS)

            @pl.when(q != 0)
            def _():
                pack(ch, q)

                @pl.when(q != o)
                def _():
                    send_blocks(ch, q).start()

        for j in range(4):
            recvs[ch][1 + 4 * o + j] = outbuf[ch, 4 * o + j]

    for ch in range(NCH):
        pack(ch, 0)

        @pl.when(o != 0)
        def _(ch=ch):
            send_blocks(ch, 0).start()

        @pl.when(o == 0)
        def _(ch=ch):
            for j in range(4):
                recvs[ch][1 + j] = outbuf[ch, j]

    send_chunk(0)

    @pl.when(o != 0)
    def _():
        for ch in range(1, NCH):
            send_chunk(ch)

    for load in small[1:]:
        load.wait()
    ids = lax.broadcasted_iota(jnp.int32, (PW, PW), 0)
    for k in range(2):
        one_hot[k] = jnp.where(piv[k : k + 1, :] == ids, 1.0, 0.0).astype(BF16)

    @pl.loop(1, NO)
    def _(k):
        q = lax.rem(o + k, NO)
        arrived(plc_in.at[q], rp.at[q])

    ip = lax.broadcasted_iota(jnp.int32, (56, BS), 0)
    lane = lax.broadcasted_iota(jnp.int32, (56, BS), 1)
    mine = (lane >= 4 * o) & (lane < 4 * o + 4)
    for half in range(2):
        found = jnp.zeros((56, BS), jnp.int32)
        for q in range(half * ZS, (half + 1) * ZS):
            hit = mine & (plc_in[q, 0:1, :] == ip)
            found = jnp.maximum(found, jnp.where(hit, 4 * q + 1 + lane - 4 * o, 0))
        src_v[half] = jnp.broadcast_to(jnp.max(found, axis=1, keepdims=True), (56, BS))
    src_load = pltpu.make_async_copy(src_v, src_s, s_idx.at[1])
    src_load.start()
    front_load.wait()
    src_load.wait()

    def add_blocks(ch, first, last):
        rows = pl.ds(ch * RC, RC)

        @pl.loop(first, last, unroll=2)
        def _(p):
            at = pl.ds(pl.multiple_of(p * BS, BS), BS)
            one = recvs[ch][src_s[0, p, 0]].astype(F32)
            two = recvs[ch][src_s[1, p, 0]].astype(F32)
            total = front_v[rows, at].astype(F32) + one + two
            work[rows, at] = total
            fb[rows, at] = total.astype(BF16)

    def wait_blocks(ch):
        @pl.loop(1, NO)
        def _(k):
            q = lax.rem(o + k, NO)
            arrived(recvs[ch].at[pl.ds(1 + 4 * q, 4)], ra.at[ch, q])

    def send_rows(ch, w, cols):
        src = fb.at[pl.ds(ch * RC, RC), pl.ds(first_col(w), cols)]
        dst = u.at[pl.ds(pl.multiple_of(r * ROWS + ch * RC, RC), RC), pl.ds(0, cols)]
        return src, dst

    def scatter(ch):
        @pl.when(r < 8)
        def _():
            @pl.loop(0, NW)
            def _(t):
                w = lax.rem(r + t, NW)

                def act(cols):
                    src, dst = send_rows(ch, w, cols)

                    @pl.when(w == r)
                    def _():
                        pltpu.make_async_copy(src, dst, rs.at[ch, lax.rem(r, 8)]).start()

                    @pl.when(w != r)
                    def _():
                        remote(src, dst, ss.at[ch, w], rs.at[ch, lax.rem(r, 8)], at_row(w)).start()

                by_width(w, act)

    rank_row = lax.broadcasted_iota(jnp.int32, (RM, BS), 0)

    def basis(k):
        return jnp.where(rank_row < ranks[0:1, k : k + 1], bases[...].astype(F32), 0.0)

    def order(k):
        ordered = nt(coef[k], one_hot[k]).astype(BF16)
        at = pl.ds(pl.multiple_of(jnp.maximum(r - 4 * (k + 1), 0) * RM, RM), RM)
        if k == 0:
            gm0[:, 0:PW] = ordered
            gm0[:, PW : PW + BS] = basis(k).astype(BF16)
        else:
            gm1[...] = ordered

        @pl.when(r >= 4 * (k + 1))
        def _():
            (g0, g1)[k][at, :] = (gm0, gm1)[k][...]

    def send_coef(k, q):
        return remote(coef.at[k], coef.at[k], sc.at[k, q], rcv.at[k], {"col": q})

    def send_pair(k):
        return remote(coef.at[k], coef.at[k], sc.at[k, 0], rcv.at[k], {"sub": 1 - s})

    def pass_coef(k):
        @pl.when(o == 0)
        def _():
            for q in (4, 5, 3, 6, 1, 7, 2):
                send_coef(k, jnp.int32(q)).start()

        @pl.when(s == 0)
        def _():
            send_pair(k).start()

    def send_panel(i):
        return remote(
            fb.at[:, pl.ds(PW, PW)], u0p.at[pl.ds(pl.multiple_of(lax.rem(r, 4) * ROWS, ROWS), ROWS), :],
            su.at[i], ru.at[lax.rem(r, 4)], at_row(i),
        )

    def slot(k, i):
        return (g0, g1)[k].at[pl.ds(pl.multiple_of((i - 4 * (k + 1)) * RM, RM), RM), :]

    def send_order(k, w):
        at = pl.ds(pl.multiple_of(jnp.maximum(r - 4 * (k + 1), 0) * RM, RM), RM)
        return remote((gm0, gm1)[k], (g0, g1)[k].at[at, :], sg.at[k, w], rg.at[k, r], at_row(w))

    def sends_order(k, w):
        return (r >= 4 * (k + 1)) & (lax.rem(r, 2) == s) & (r != w)

    def share(k):
        @pl.loop(1, NW)
        def _(t):
            w = lax.rem(r + t, NW)

            @pl.when(sends_order(k, w))
            def _():
                send_order(k, w).start()

    def send_sibling(k, i):
        return remote(slot(k, i), slot(k, i), sf.at[k, i], rg.at[k, i], {"sub": 1 - s})

    def exchange(k):
        @pl.loop(4 * (k + 1), 16)
        def _(i):
            @pl.when((r != i) & (s == lax.rem(i, 2)))
            def _():
                arrived(slot(k, i), rg.at[k, i])
                send_sibling(k, i).start()

    def exchanged(k):
        @pl.loop(4 * (k + 1), 16)
        def _(i):
            @pl.when((r != i) & (s != lax.rem(i, 2)))
            def _():
                arrived(slot(k, i), rg.at[k, i])

    @pl.when(o == 0)
    def _():
        for ch in range(NCH):
            wait_blocks(ch)
        for ch in range(NCH):
            add_blocks(ch, 0, 8)

        @pl.when(r < 4)
        def _():
            @pl.loop(4, 16)
            def _(i):
                send_panel(i).start()

        inv_load.wait()
        coef[0] = mm_high(mm_high(basis(0), work[:, 0:PW]), inv_v[0]).astype(BF16)
        pass_coef(0)
        order(0)
        share(0)
        send_chunk(1)
        send_chunk(2)
        for ch in range(NCH):
            add_blocks(ch, 8, PB)
            scatter(ch)
        p1[...] = work[:, PW : 2 * PW]

        @pl.when(r >= 4)
        def _():
            for i in range(4):
                arrived(u0p.at[pl.ds(i * ROWS, ROWS), :], ru.at[i])
            reduced = mm(gm0[:, 0:PW], u0p[...]).astype(BF16)
            p1[...] = p1[...] - mm(transposed(basis(0)).astype(BF16), reduced)

        coef[1] = mm_high(mm_high(basis(1), p1[...]), inv_v[1]).astype(BF16)
        pass_coef(1)
        send_chunk(3)
        order(1)
        share(1)
        exchange(0)

    @pl.when(o != 0)
    def _():
        inv_load.wait()
        arrived(coef.at[0], rcv.at[0])
        pass_coef(0)
        order(0)
        share(0)

        @pl.when(r < 8)
        def _():
            for ch in range(NCH - 1):
                wait_blocks(ch)
                add_blocks(ch, 0, PB)
                scatter(ch)

        exchange(0)

        @pl.when(r < 8)
        def _():
            wait_blocks(NCH - 1)
            add_blocks(NCH - 1, 0, PB)
            scatter(NCH - 1)

        arrived(coef.at[1], rcv.at[1])
        pass_coef(1)
        order(1)
        share(1)

    coef_copy = pltpu.make_async_copy(coef, coef_out.at[:, 0], s_coef)
    coef_copy.start()

    def got_rows(first, last):
        def act(cols):
            @pl.loop(first, last)
            def _(i):
                for ch in range(NCH):
                    rows = pl.ds(pl.multiple_of(i * ROWS + ch * RC, RC), RC)
                    arrived(u.at[rows, pl.ds(0, cols)], rs.at[ch, i])

        by_width(r, act)

    def send_reduced(k, i, cols):
        src = (r0, r1)[k].at[pl.ds(pl.multiple_of((i - 4 * (k + 1)) * RM, RM), RM), pl.ds(0, cols)]
        dst = rbuf.at[pl.ds(k * RM, RM), pl.ds(first_col(r), cols)]
        return src, dst

    def give(k, first):
        def act(cols):
            @pl.loop(0, 4)
            def _(t):
                i = first + lax.rem(r + t, 4)
                src, dst = send_reduced(k, i, cols)

                @pl.when(r == i)
                def _():
                    pltpu.make_async_copy(src, dst, rr.at[k, r]).start()

                @pl.when(r != i)
                def _():
                    remote(src, dst, sr.at[k, i], rr.at[k, r], at_row(i)).start()

        by_width(r, act)

    exchanged(0)
    got_rows(0, 4)

    @pl.loop(0, 3)
    def _(t):
        at = pl.ds(pl.multiple_of(t * 256, 256), 256)
        r0[at, :] = mm(g0[at, 0:PW], u[0:PW, :]).astype(BF16)
        give(0, 4 + 4 * t)

    exchange(1)
    got_rows(4, 8)

    @pl.loop(0, 4)
    def _(i):
        ranks_at = pl.ds(pl.multiple_of(i * RM, RM), RM)
        b_t = transposed(g0[ranks_at, PW : PW + BS]).astype(BF16)
        rows = pl.ds(pl.multiple_of(PW + i * ROWS, ROWS), ROWS)
        u[rows, :] = (u[rows, :].astype(F32) - mm(b_t, r0[ranks_at, :])).astype(BF16)

    exchanged(1)

    @pl.loop(0, 2)
    def _(t):
        at = pl.ds(pl.multiple_of(t * 256, 256), 256)
        r1[at, :] = mm(g1[at, :], u[PW : 2 * PW, :]).astype(BF16)
        give(1, 8 + 4 * t)

    @pl.when((o != 0) & (r >= 8))
    def _():
        for ch in range(NCH):
            wait_blocks(ch)
            add_blocks(ch, 0, PB)

    @pl.loop(1, NO)
    def _(k):
        q = lax.rem(o + k, NO)
        send_places(q).wait_send()
        for ch in range(NCH):
            send_blocks(ch, q).wait_send()

    @pl.when((o == 0) & (r < 4))
    def _():
        @pl.loop(4, 16)
        def _(i):
            send_panel(i).wait_send()

    for k in range(2):

        @pl.when(o == 0)
        def _():
            @pl.loop(1, ZS)
            def _(q):
                send_coef(k, q).wait_send()

        @pl.when(s == 0)
        def _():
            send_pair(k).wait_send()

        @pl.loop(0, NW)
        def _(w):
            @pl.when(sends_order(k, w))
            def _():
                send_order(k, w).wait_send()

        @pl.loop(4 * (k + 1), 16)
        def _(i):
            @pl.when((r != i) & (s == lax.rem(i, 2)))
            def _():
                send_sibling(k, i).wait_send()

    @pl.when(r < 8)
    def _():
        @pl.loop(1, NW)
        def _(t):
            w = lax.rem(r + t, NW)

            def act(cols):
                for ch in range(NCH):
                    src, dst = send_rows(ch, w, cols)
                    remote(src, dst, ss.at[ch, w], rs.at[ch, lax.rem(r, 8)], at_row(w)).wait_send()

            by_width(w, act)

    def each_part(act):
        @pl.loop(0, NW)
        def _(w):
            by_width(w, lambda cols: act(w, cols))

    def write(w, cols, src):
        at = pl.ds(first_col(w), cols)
        return pltpu.make_async_copy(src.at[:, at], out.at[:, at], so.at[w])

    @pl.when(r < 4)
    def _():
        each_part(lambda w, cols: write(w, cols, fb).start())

    def apply(count):
        b_t = transposed(jnp.concatenate([basis(0), basis(1)][:count], axis=0)).astype(BF16)

        def act(w, cols):
            at = pl.ds(first_col(w), cols)
            for k in range(count):
                arrived(rbuf.at[pl.ds(k * RM, RM), at], rr.at[k, w])
            outv[:, at] = (work[:, at] - mm(b_t, rbuf[0 : count * RM, at])).astype(BF16)
            write(w, cols, outv).start()

        each_part(act)

    @pl.when((r >= 4) & (r < 8))
    def _():
        apply(1)

    @pl.when(r >= 8)
    def _():
        apply(2)

    each_part(lambda w, cols: write(w, cols, outv).wait())
    coef_copy.wait()

    for k in range(2):

        def sent(cols, k=k):
            @pl.loop(4 * (k + 1), 16)
            def _(i):
                src, dst = send_reduced(k, i, cols)

                @pl.when(r != i)
                def _():
                    remote(src, dst, sr.at[k, i], rr.at[k, r], at_row(i)).wait_send()

        by_width(r, sent)


def local(front, child_update, col_map, pivots, diag_inverse, ranks, bases):
    anywhere = pl.BlockSpec(memory_space=pl.ANY)
    dma = pltpu.SemaphoreType.DMA
    scratch = [
        pltpu.VMEM((1, KB), jnp.int32),
        pltpu.VMEM((2, PW), jnp.int32),
        pltpu.VMEM((1, 2), jnp.int32),
        pltpu.VMEM((RM, BS), BF16),
        pltpu.VMEM((2, PW, PW), BF16),
        pltpu.VMEM((NCH, RC, KB * BS), BF16),
        [pltpu.VMEM((KB, RC, BS), BF16) for _ in range(NCH)],
        pltpu.VMEM((ROWS, COLS), BF16),
        pltpu.VMEM((2, PW, PW), F32),
        pltpu.VMEM((NCH, KB, RC, BS), BF16),
        [pltpu.VMEM((KB + 1, RC, BS), BF16) for _ in range(NCH)],
        pltpu.VMEM((8, BS), jnp.int32),
        pltpu.VMEM((NO, 8, BS), jnp.int32),
        pltpu.VMEM((8, BS), jnp.int32),
        pltpu.SMEM((8, BS), jnp.int32),
        pltpu.VMEM((2, 56, BS), jnp.int32),
        pltpu.SMEM((2, 56, BS), jnp.int32),
        pltpu.VMEM((ROWS, COLS), F32),
        pltpu.VMEM((ROWS, COLS), BF16),
        pltpu.VMEM((ROWS, PW), F32),
        pltpu.VMEM((PW, PW), BF16),
        pltpu.VMEM((2, RM, PW), BF16),
        pltpu.VMEM((RM, PW + BS), BF16),
        pltpu.VMEM((RM, PW), BF16),
        pltpu.VMEM((12 * RM, PW + BS), BF16),
        pltpu.VMEM((8 * RM, PW), BF16),
        pltpu.VMEM((2 * PW, WC), BF16),
        pltpu.VMEM((12 * RM, WC), BF16),
        pltpu.VMEM((8 * RM, WC), BF16),
        pltpu.VMEM((2 * RM, COLS), BF16),
        pltpu.VMEM((ROWS, COLS), BF16),
        dma((NCH,)), dma((6,)), dma((2,)),
        dma((NCH, NO)), dma((NCH, NO)), dma((NO,)), dma((NO,)),
        dma((16,)), dma((4,)),
        dma((2, 8)), dma((2,)),
        dma((2, NW)), dma((2, 16)), dma((2, 16)),
        dma((NCH, NW)), dma((NCH, 8)),
        dma((2, 16)), dma((2, NW)),
        dma((NW,)), dma(()),
    ]
    return pl.pallas_call(
        kernel,
        out_shape=(
            jax.ShapeDtypeStruct((ROWS, COLS), BF16),
            jax.ShapeDtypeStruct((2, 1, RM, PW), BF16),
        ),
        in_specs=[anywhere] * 7,
        out_specs=(anywhere, anywhere),
        scratch_shapes=scratch,
        compiler_params=pltpu.CompilerParams(
            collective_id=0, has_side_effects=True, vmem_limit_bytes=60 * 1024 * 1024
        ),
        cost_estimate=pl.CostEstimate(flops=1_200_000_000, bytes_accessed=8_000_000, transcendentals=0),
    )(col_map.reshape(1, KB), pivots, ranks.reshape(1, 2), bases, child_update, front, diag_inverse)


def solution(mesh):
    return jax.shard_map(
        local,
        mesh=mesh,
        in_specs=(
            P("row", ("sub", "col")),
            P("row", ("sub", "col")),
            P(("sub", "col")),
            P(),
            P(),
            P(None, "row"),
            P(None, "row"),
        ),
        out_specs=(P("row", ("sub", "col")), P(None, "row", None, None)),
        check_vma=False,
    )
```

```python
import functools

import jax
import jax.numpy as jnp
from jax import lax
from jax.experimental import pallas as pl
from jax.experimental.pallas import tpu as pltpu
from jax.sharding import PartitionSpec as P

BS = 128
PW = 512
RM = 64
ROWS = 128
COLS = 6400
PB = 50
KB = 64
NO = 16
ZS = 8
NCH = 4
RC = ROWS // NCH
NW = 16
SHARES = ((0, 4, 2), (4, 8, 3), (8, 14, 4), (14, 16, 3))
WC = 4 * BS
F32 = jnp.float32
BF16 = jnp.bfloat16
HIGH = lax.Precision.HIGHEST


def first_col(w):
    first, before = 0, 0
    for start, end, blocks in SHARES:
        first = jnp.where(w >= start, before + (w - start) * blocks, first)
        before += (end - start) * blocks
    return pl.multiple_of(first * BS, BS)


def by_width(w, act):
    for blocks in sorted({share[2] for share in SHARES}):
        mine = w < 0
        for start, end, count in SHARES:
            if count == blocks:
                mine = mine | ((w >= start) & (w < end))

        @pl.when(mine)
        def _():
            act(blocks * BS)


def nt(a, b):
    return lax.dot_general(a, b, (((1,), (1,)), ((), ())), preferred_element_type=F32)


def mm(a, b):
    return jnp.dot(a, b, preferred_element_type=F32)


def mm_high(a, b):
    return jnp.dot(a, b, preferred_element_type=F32, precision=HIGH)


def transposed(a):
    return a.astype(F32).T


def kernel(
    cm_h, piv_h, ranks_h, bases_h, child, front, inv, out, coef_out,
    cm, piv, ranks, bases, one_hot, child_v, childs, front_v, inv_v, outbuf, recvs, plc_out, plc_in, arr_v, arr_s, src_v, src_s,
    work, fb, p1, u0p, coef, gm0, gm1, g0, g1, u, r0, r1, rbuf, outv,
    s_child, s_load, s_idx, sa, ra, sp, rp, su, ru, sc, rcv, sg, rg, sf, ss, rs, sr, rr, so, s_coef,
):
    s, r, c = lax.axis_index("sub"), lax.axis_index("row"), lax.axis_index("col")
    o = s * ZS + c

    def at_owner(q):
        return {"sub": q // ZS, "col": lax.rem(q, ZS)}

    def at_row(i):
        return {"row": i}

    def remote(src, dst, send, recv, dev):
        return pltpu.make_async_remote_copy(
            src_ref=src, dst_ref=dst, send_sem=send, recv_sem=recv, device_id=dev,
            device_id_type=pl.DeviceIdType.MESH,
        )

    def arrived(dst, sem):
        pltpu.make_async_copy(dst, dst, sem).wait()

    small = []
    for i, (src, dst) in enumerate(((cm_h, cm), (piv_h, piv), (ranks_h, ranks), (bases_h, bases))):
        small.append(pltpu.make_async_copy(src, dst, s_load.at[2 + i]))
        small[-1].start()
    loads = []
    for ch in range(NCH):
        rows = pl.ds(ch * RC, RC)
        loads.append(pltpu.make_async_copy(child.at[rows, :], child_v.at[ch], s_child.at[ch]))
        loads[-1].start()
    front_load = pltpu.make_async_copy(front, front_v, s_load.at[0])
    front_load.start()
    inv_load = pltpu.make_async_copy(inv, inv_v, s_load.at[1])
    inv_load.start()

    barrier = pltpu.get_barrier_semaphore()

    @pl.loop(1, 16)
    def _(k):
        pl.semaphore_signal(
            barrier, inc=1, device_id=at_owner(lax.rem(o + k, NO)), device_id_type=pl.DeviceIdType.MESH
        )
        pl.semaphore_signal(
            barrier, inc=1, device_id=at_row(lax.rem(r + k, 16)), device_id_type=pl.DeviceIdType.MESH
        )

    small[0].wait()
    i0 = lax.broadcasted_iota(jnp.int32, (KB, KB), 0)
    i1 = lax.broadcasted_iota(jnp.int32, (KB, KB), 1)
    along = jnp.broadcast_to(cm[...], (KB, KB))
    down = jnp.sum(jnp.where(i0 == i1, along, 0), axis=1, keepdims=True)
    t_along = (along * 1311) >> 16
    t_down = (down * 1311) >> 16
    slot = jnp.sum(jnp.where((t_along == t_down) & (i1 < i0), 1, 0), axis=1, keepdims=True)
    match = (4 * t_down + slot) == i1
    arrange = jnp.max(jnp.where(match, i0, 0), axis=0, keepdims=True)
    places = jnp.sum(jnp.where(match, down - PB * t_down, 0), axis=0, keepdims=True)
    arr_v[...] = jnp.zeros_like(arr_v)
    arr_v[:, 0:KB] = jnp.broadcast_to(arrange, (8, KB))
    plc_out[...] = jnp.zeros_like(plc_out)
    plc_out[:, 0:KB] = jnp.broadcast_to(places, (8, KB))
    idx_load = pltpu.make_async_copy(arr_v, arr_s, s_idx.at[0])
    idx_load.start()
    plc_in[o] = plc_out[...]
    for ch in range(NCH):
        recvs[ch][0] = jnp.zeros((RC, BS), BF16)
    idx_load.wait()
    pl.semaphore_wait(barrier, 30)

    def send_places(q):
        return remote(plc_out, plc_in.at[o], sp.at[q], rp.at[o], at_owner(q))

    def send_blocks(ch, q):
        return remote(
            outbuf.at[ch, pl.ds(4 * q, 4)], recvs[ch].at[pl.ds(1 + 4 * o, 4)], sa.at[ch, q], ra.at[ch, o],
            at_owner(q),
        )

    def pack(ch, q):
        for j in range(4):
            outbuf[ch, 4 * q + j] = childs[ch][arr_s[0, 4 * q + j]]

    @pl.loop(1, NO)
    def _(k):
        send_places(lax.rem(o + k, NO)).start()

    for ch in range(NCH):
        loads[ch].wait()

        @pl.loop(0, KB, unroll=8)
        def _(j, ch=ch):
            childs[ch][j] = child_v[ch, :, pl.ds(pl.multiple_of(j * BS, BS), BS)]

    def send_chunk(ch):
        @pl.loop(0, NO)
        def _(t):
            step = t // 2
            base = 0 if ch == NCH - 1 else ZS // 2
            shift = jnp.where(lax.rem(step, 2) == 1, base + (step + 1) // 2, base + ZS - step // 2)
            q = lax.rem(s + lax.rem(t, 2), 2) * ZS + lax.rem(c + shift, ZS)

            @pl.when(q != 0)
            def _():
                pack(ch, q)

                @pl.when(q != o)
                def _():
                    send_blocks(ch, q).start()

        for j in range(4):
            recvs[ch][1 + 4 * o + j] = outbuf[ch, 4 * o + j]

    for ch in range(NCH):
        pack(ch, 0)

        @pl.when(o != 0)
        def _(ch=ch):
            send_blocks(ch, 0).start()

        @pl.when(o == 0)
        def _(ch=ch):
            for j in range(4):
                recvs[ch][1 + j] = outbuf[ch, j]

    send_chunk(0)

    @pl.when(o != 0)
    def _():
        for ch in range(1, NCH):
            send_chunk(ch)

    for load in small[1:]:
        load.wait()
    ids = lax.broadcasted_iota(jnp.int32, (PW, PW), 0)
    for k in range(2):
        one_hot[k] = jnp.where(piv[k : k + 1, :] == ids, 1.0, 0.0).astype(BF16)

    @pl.loop(1, NO)
    def _(k):
        q = lax.rem(o + k, NO)
        arrived(plc_in.at[q], rp.at[q])

    ip = lax.broadcasted_iota(jnp.int32, (56, BS), 0)
    lane = lax.broadcasted_iota(jnp.int32, (56, BS), 1)
    mine = (lane >= 4 * o) & (lane < 4 * o + 4)
    for half in range(2):
        found = jnp.zeros((56, BS), jnp.int32)
        for q in range(half * ZS, (half + 1) * ZS):
            hit = mine & (plc_in[q, 0:1, :] == ip)
            found = jnp.maximum(found, jnp.where(hit, 4 * q + 1 + lane - 4 * o, 0))
        src_v[half] = jnp.broadcast_to(jnp.max(found, axis=1, keepdims=True), (56, BS))
    src_load = pltpu.make_async_copy(src_v, src_s, s_idx.at[1])
    src_load.start()
    front_load.wait()
    src_load.wait()

    def add_blocks(ch, first, last):
        rows = pl.ds(ch * RC, RC)

        @pl.loop(first, last, unroll=2)
        def _(p):
            at = pl.ds(pl.multiple_of(p * BS, BS), BS)
            one = recvs[ch][src_s[0, p, 0]].astype(F32)
            two = recvs[ch][src_s[1, p, 0]].astype(F32)
            total = front_v[rows, at].astype(F32) + one + two
            work[rows, at] = total
            fb[rows, at] = total.astype(BF16)

    def wait_blocks(ch):
        @pl.loop(1, NO)
        def _(k):
            q = lax.rem(o + k, NO)
            arrived(recvs[ch].at[pl.ds(1 + 4 * q, 4)], ra.at[ch, q])

    def send_rows(ch, w, cols):
        src = fb.at[pl.ds(ch * RC, RC), pl.ds(first_col(w), cols)]
        dst = u.at[pl.ds(pl.multiple_of(r * ROWS + ch * RC, RC), RC), pl.ds(0, cols)]
        return src, dst

    def scatter(ch):
        @pl.when(r < 8)
        def _():
            @pl.loop(0, NW)
            def _(t):
                w = lax.rem(r + t, NW)

                def act(cols):
                    src, dst = send_rows(ch, w, cols)

                    @pl.when(w == r)
                    def _():
                        pltpu.make_async_copy(src, dst, rs.at[ch, lax.rem(r, 8)]).start()

                    @pl.when(w != r)
                    def _():
                        remote(src, dst, ss.at[ch, w], rs.at[ch, lax.rem(r, 8)], at_row(w)).start()

                by_width(w, act)

    rank_row = lax.broadcasted_iota(jnp.int32, (RM, BS), 0)

    def basis(k):
        return jnp.where(rank_row < ranks[0:1, k : k + 1], bases[...].astype(F32), 0.0)

    def order(k):
        ordered = nt(coef[k], one_hot[k]).astype(BF16)
        at = pl.ds(pl.multiple_of(jnp.maximum(r - 4 * (k + 1), 0) * RM, RM), RM)
        if k == 0:
            gm0[:, 0:PW] = ordered
            gm0[:, PW : PW + BS] = basis(k).astype(BF16)
        else:
            gm1[...] = ordered

        @pl.when(r >= 4 * (k + 1))
        def _():
            (g0, g1)[k][at, :] = (gm0, gm1)[k][...]

    def send_coef(k, q):
        return remote(coef.at[k], coef.at[k], sc.at[k, q], rcv.at[k], {"col": q})

    def send_pair(k):
        return remote(coef.at[k], coef.at[k], sc.at[k, 0], rcv.at[k], {"sub": 1 - s})

    def pass_coef(k):
        @pl.when(o == 0)
        def _():
            for q in (4, 5, 3, 6, 1, 7, 2):
                send_coef(k, jnp.int32(q)).start()

        @pl.when(s == 0)
        def _():
            send_pair(k).start()

    def send_panel(i):
        return remote(
            fb.at[:, pl.ds(PW, PW)], u0p.at[pl.ds(pl.multiple_of(lax.rem(r, 4) * ROWS, ROWS), ROWS), :],
            su.at[i], ru.at[lax.rem(r, 4)], at_row(i),
        )

    def slot(k, i):
        return (g0, g1)[k].at[pl.ds(pl.multiple_of((i - 4 * (k + 1)) * RM, RM), RM), :]

    def send_order(k, w):
        at = pl.ds(pl.multiple_of(jnp.maximum(r - 4 * (k + 1), 0) * RM, RM), RM)
        return remote((gm0, gm1)[k], (g0, g1)[k].at[at, :], sg.at[k, w], rg.at[k, r], at_row(w))

    def sends_order(k, w):
        return (r >= 4 * (k + 1)) & (lax.rem(r, 2) == s) & (r != w)

    def share(k):
        @pl.loop(1, NW)
        def _(t):
            w = lax.rem(r + t, NW)

            @pl.when(sends_order(k, w))
            def _():
                send_order(k, w).start()

    def send_sibling(k, i):
        return remote(slot(k, i), slot(k, i), sf.at[k, i], rg.at[k, i], {"sub": 1 - s})

    def exchange(k):
        @pl.loop(4 * (k + 1), 16)
        def _(i):
            @pl.when((r != i) & (s == lax.rem(i, 2)))
            def _():
                arrived(slot(k, i), rg.at[k, i])
                send_sibling(k, i).start()

    def exchanged(k):
        @pl.loop(4 * (k + 1), 16)
        def _(i):
            @pl.when((r != i) & (s != lax.rem(i, 2)))
            def _():
                arrived(slot(k, i), rg.at[k, i])

    @pl.when(o == 0)
    def _():
        for ch in range(NCH):
            wait_blocks(ch)
        for ch in range(NCH):
            add_blocks(ch, 0, 8)

        @pl.when(r < 4)
        def _():
            @pl.loop(4, 16)
            def _(i):
                send_panel(i).start()

        inv_load.wait()
        coef[0] = mm_high(mm_high(basis(0), work[:, 0:PW]), inv_v[0]).astype(BF16)
        pass_coef(0)
        order(0)
        share(0)
        send_chunk(1)
        send_chunk(2)
        for ch in range(NCH):
            add_blocks(ch, 8, PB)
            scatter(ch)
        p1[...] = work[:, PW : 2 * PW]

        @pl.when(r >= 4)
        def _():
            for i in range(4):
                arrived(u0p.at[pl.ds(i * ROWS, ROWS), :], ru.at[i])
            reduced = mm(gm0[:, 0:PW], u0p[...]).astype(BF16)
            p1[...] = p1[...] - mm(transposed(basis(0)).astype(BF16), reduced)

        coef[1] = mm_high(mm_high(basis(1), p1[...]), inv_v[1]).astype(BF16)
        pass_coef(1)
        send_chunk(3)
        order(1)
        share(1)
        exchange(0)

    @pl.when(o != 0)
    def _():
        inv_load.wait()
        arrived(coef.at[0], rcv.at[0])
        pass_coef(0)
        order(0)
        share(0)

        @pl.when(r < 8)
        def _():
            for ch in range(NCH - 1):
                wait_blocks(ch)
                add_blocks(ch, 0, PB)
                scatter(ch)

        exchange(0)

        @pl.when(r < 8)
        def _():
            wait_blocks(NCH - 1)
            add_blocks(NCH - 1, 0, PB)
            scatter(NCH - 1)

        arrived(coef.at[1], rcv.at[1])
        pass_coef(1)
        order(1)
        share(1)

    coef_copy = pltpu.make_async_copy(coef, coef_out.at[:, 0], s_coef)
    coef_copy.start()

    def got_rows(first, last):
        def act(cols):
            @pl.loop(first, last)
            def _(i):
                for ch in range(NCH):
                    rows = pl.ds(pl.multiple_of(i * ROWS + ch * RC, RC), RC)
                    arrived(u.at[rows, pl.ds(0, cols)], rs.at[ch, i])

        by_width(r, act)

    def send_reduced(k, i, cols):
        src = (r0, r1)[k].at[pl.ds(pl.multiple_of((i - 4 * (k + 1)) * RM, RM), RM), pl.ds(0, cols)]
        dst = rbuf.at[pl.ds(k * RM, RM), pl.ds(first_col(r), cols)]
        return src, dst

    def give(k, first):
        def act(cols):
            @pl.loop(0, 4)
            def _(t):
                i = first + lax.rem(r + t, 4)
                src, dst = send_reduced(k, i, cols)

                @pl.when(r == i)
                def _():
                    pltpu.make_async_copy(src, dst, rr.at[k, r]).start()

                @pl.when(r != i)
                def _():
                    remote(src, dst, sr.at[k, i], rr.at[k, r], at_row(i)).start()

        by_width(r, act)

    exchanged(0)
    got_rows(0, 4)

    @pl.loop(0, 3)
    def _(t):
        at = pl.ds(pl.multiple_of(t * 256, 256), 256)
        r0[at, :] = mm(g0[at, 0:PW], u[0:PW, :]).astype(BF16)
        give(0, 4 + 4 * t)

    exchange(1)
    got_rows(4, 8)

    @pl.loop(0, 4)
    def _(i):
        ranks_at = pl.ds(pl.multiple_of(i * RM, RM), RM)
        b_t = transposed(g0[ranks_at, PW : PW + BS]).astype(BF16)
        rows = pl.ds(pl.multiple_of(PW + i * ROWS, ROWS), ROWS)
        u[rows, :] = (u[rows, :].astype(F32) - mm(b_t, r0[ranks_at, :])).astype(BF16)

    exchanged(1)

    @pl.loop(0, 2)
    def _(t):
        at = pl.ds(pl.multiple_of(t * 256, 256), 256)
        r1[at, :] = mm(g1[at, :], u[PW : 2 * PW, :]).astype(BF16)
        give(1, 8 + 4 * t)

    @pl.when((o != 0) & (r >= 8))
    def _():
        for ch in range(NCH):
            wait_blocks(ch)
            add_blocks(ch, 0, PB)

    @pl.loop(1, NO)
    def _(k):
        q = lax.rem(o + k, NO)
        send_places(q).wait_send()
        for ch in range(NCH):
            send_blocks(ch, q).wait_send()

    @pl.when((o == 0) & (r < 4))
    def _():
        @pl.loop(4, 16)
        def _(i):
            send_panel(i).wait_send()

    for k in range(2):

        @pl.when(o == 0)
        def _():
            @pl.loop(1, ZS)
            def _(q):
                send_coef(k, q).wait_send()

        @pl.when(s == 0)
        def _():
            send_pair(k).wait_send()

        @pl.loop(0, NW)
        def _(w):
            @pl.when(sends_order(k, w))
            def _():
                send_order(k, w).wait_send()

        @pl.loop(4 * (k + 1), 16)
        def _(i):
            @pl.when((r != i) & (s == lax.rem(i, 2)))
            def _():
                send_sibling(k, i).wait_send()

    @pl.when(r < 8)
    def _():
        @pl.loop(1, NW)
        def _(t):
            w = lax.rem(r + t, NW)

            def act(cols):
                for ch in range(NCH):
                    src, dst = send_rows(ch, w, cols)
                    remote(src, dst, ss.at[ch, w], rs.at[ch, lax.rem(r, 8)], at_row(w)).wait_send()

            by_width(w, act)

    def each_part(act):
        @pl.loop(0, NW)
        def _(w):
            by_width(w, lambda cols: act(w, cols))

    def write(w, cols, src):
        at = pl.ds(first_col(w), cols)
        return pltpu.make_async_copy(src.at[:, at], out.at[:, at], so.at[w])

    @pl.when(r < 4)
    def _():
        each_part(lambda w, cols: write(w, cols, fb).start())

    def apply(count):
        b_t = transposed(jnp.concatenate([basis(0), basis(1)][:count], axis=0)).astype(BF16)

        def act(w, cols):
            at = pl.ds(first_col(w), cols)
            for k in range(count):
                arrived(rbuf.at[pl.ds(k * RM, RM), at], rr.at[k, w])
            outv[:, at] = (work[:, at] - mm(b_t, rbuf[0 : count * RM, at])).astype(BF16)
            write(w, cols, outv).start()

        each_part(act)

    @pl.when((r >= 4) & (r < 8))
    def _():
        apply(1)

    @pl.when(r >= 8)
    def _():
        apply(2)

    each_part(lambda w, cols: write(w, cols, outv).wait())
    coef_copy.wait()

    for k in range(2):

        def sent(cols, k=k):
            @pl.loop(4 * (k + 1), 16)
            def _(i):
                src, dst = send_reduced(k, i, cols)

                @pl.when(r != i)
                def _():
                    remote(src, dst, sr.at[k, i], rr.at[k, r], at_row(i)).wait_send()

        by_width(r, sent)


def local(front, child_update, col_map, pivots, diag_inverse, ranks, bases):
    anywhere = pl.BlockSpec(memory_space=pl.ANY)
    dma = pltpu.SemaphoreType.DMA
    scratch = [
        pltpu.VMEM((1, KB), jnp.int32),
        pltpu.VMEM((2, PW), jnp.int32),
        pltpu.VMEM((1, 2), jnp.int32),
        pltpu.VMEM((RM, BS), BF16),
        pltpu.VMEM((2, PW, PW), BF16),
        pltpu.VMEM((NCH, RC, KB * BS), BF16),
        [pltpu.VMEM((KB, RC, BS), BF16) for _ in range(NCH)],
        pltpu.VMEM((ROWS, COLS), BF16),
        pltpu.VMEM((2, PW, PW), F32),
        pltpu.VMEM((NCH, KB, RC, BS), BF16),
        [pltpu.VMEM((KB + 1, RC, BS), BF16) for _ in range(NCH)],
        pltpu.VMEM((8, BS), jnp.int32),
        pltpu.VMEM((NO, 8, BS), jnp.int32),
        pltpu.VMEM((8, BS), jnp.int32),
        pltpu.SMEM((8, BS), jnp.int32),
        pltpu.VMEM((2, 56, BS), jnp.int32),
        pltpu.SMEM((2, 56, BS), jnp.int32),
        pltpu.VMEM((ROWS, COLS), F32),
        pltpu.VMEM((ROWS, COLS), BF16),
        pltpu.VMEM((ROWS, PW), F32),
        pltpu.VMEM((PW, PW), BF16),
        pltpu.VMEM((2, RM, PW), BF16),
        pltpu.VMEM((RM, PW + BS), BF16),
        pltpu.VMEM((RM, PW), BF16),
        pltpu.VMEM((12 * RM, PW + BS), BF16),
        pltpu.VMEM((8 * RM, PW), BF16),
        pltpu.VMEM((2 * PW, WC), BF16),
        pltpu.VMEM((12 * RM, WC), BF16),
        pltpu.VMEM((8 * RM, WC), BF16),
        pltpu.VMEM((2 * RM, COLS), BF16),
        pltpu.VMEM((ROWS, COLS), BF16),
        dma((NCH,)), dma((6,)), dma((2,)),
        dma((NCH, NO)), dma((NCH, NO)), dma((NO,)), dma((NO,)),
        dma((16,)), dma((4,)),
        dma((2, 8)), dma((2,)),
        dma((2, NW)), dma((2, 16)), dma((2, 16)),
        dma((NCH, NW)), dma((NCH, 8)),
        dma((2, 16)), dma((2, NW)),
        dma((NW,)), dma(()),
    ]
    return pl.pallas_call(
        kernel,
        out_shape=(
            jax.ShapeDtypeStruct((ROWS, COLS), BF16),
            jax.ShapeDtypeStruct((2, 1, RM, PW), BF16),
        ),
        in_specs=[anywhere] * 7,
        out_specs=(anywhere, anywhere),
        scratch_shapes=scratch,
        compiler_params=pltpu.CompilerParams(
            collective_id=0, has_side_effects=True, vmem_limit_bytes=60 * 1024 * 1024
        ),
        cost_estimate=pl.CostEstimate(flops=1_200_000_000, bytes_accessed=8_000_000, transcendentals=0),
    )(col_map.reshape(1, KB), pivots, ranks.reshape(1, 2), bases, child_update, front, diag_inverse)


def solution(mesh):
    return jax.shard_map(
        local,
        mesh=mesh,
        in_specs=(
            P("row", ("sub", "col")),
            P("row", ("sub", "col")),
            P(("sub", "col")),
            P(),
            P(),
            P(None, "row"),
            P(None, "row"),
        ),
        out_specs=(P("row", ("sub", "col")), P(None, "row", None, None)),
        check_vma=False,
    )
```
